128 devices in a mesh: dp: 4 (over z_lo, core), seq: 32 (over x, z_hi, y).
Axes of the slice: x: 4, y: 4, z: 4 (z_hi: 2, z_lo: 2; z = z_hi * 2 + z_lo), core: 2. Of those that a mesh axis runs over, the one named last changes fastest.
Arguments:
- latents: bfloat16 [4, 16, 512, 1152], P('dp', None, 'seq'), may hold values from -40 to 40
- shift_mod: bfloat16 [4, 1152], P('dp'), may hold values from -2.5 to 2.5
- scale_mod: bfloat16 [4, 1152], P('dp'), may hold values from -2.5 to 2.5
- gate_mod: bfloat16 [4, 1152], P('dp'), may hold values from 0.5 to 1.5
- qkv_weight: bfloat16 [1152, 3456], replicated, may hold values from -16 to 16
- out_weight: bfloat16 [1152, 1152], replicated, may hold values from -0.1875 to 0.1875
- cotangent: bfloat16 [4, 16, 512, 1152], P('dp', None, 'seq'), may hold values from -6 to 6
Outputs:
- block_out: bfloat16 [4, 16, 512, 1152], P('dp', None, 'seq')
- latent_grad: bfloat16 [4, 16, 512, 1152], P('dp', None, 'seq')
- qkv_weight_grad: float32 [1152, 3456], P(('dp', 'seq'))
- out_weight_grad: float32 [1152, 1152], P(('dp', 'seq'))
The draws below stay inside these ranges and needn't reach their ends.
All inputs are finite; a program needn't handle non-finite values.
Results may differ from the reference program's by a relative error of at most 0.022.
The reference program's roundings to bfloat16 on the way count: a program that leaves them out, or rounds other values in their place, can miss the bound.
Values may be sent and summed in bfloat16 or wider, within the bound.
A program may use at most 128 MiB of HBM per device.

```python
import math
import jax
import jax.numpy as jnp
from jax import lax

D = 1152
H = 16
HD = 72
F = 16
P_SIZE = 512
B = 4


def draw_latents(key, part):
    key = jax.random.fold_in(key, 11)
    first = jax.random.fold_in(key, 0)
    values = jax.random.truncated_normal(first, -4.0, 4.0, (B, F, P_SIZE, D), jnp.float32)
    return values.astype(jnp.bfloat16)


def draw_qkv_weight(key, part):
    key = jax.random.fold_in(key, 12)
    first = jax.random.fold_in(key, 0)
    values = jax.random.truncated_normal(first, -4.0, 4.0, (D, 3, H, HD), jnp.float32) * D ** (-0.5)
    return values.reshape(D, 3 * D).astype(jnp.bfloat16)


def block_scale(key, extent, cuts, smallest, top_value):
    loudness = 1.0
    for axis_at, blocks in cuts:
        steps = jax.random.uniform(jax.random.fold_in(jax.random.fold_in(key, 6), axis_at), (blocks,), jnp.float32, smallest / len(cuts), top_value / len(cuts))
        loudness = loudness * jnp.repeat(jnp.exp(steps), extent[axis_at] // blocks).reshape((-1,) + (1,) * (len(extent) - 1 - axis_at))
    return loudness


def scatter_about(own_key, shape, scale, reach, cuts=(), held_as=jnp.bfloat16):
    values = jax.random.normal(own_key, shape, jnp.float32) * scale
    if len(cuts) > 0:
        values = block_scale(own_key, shape, cuts, -0.22, 0.18) * values
    return jnp.clip(values, min=-reach, max=reach).astype(held_as)


def setup_inputs(seed: int = 0) -> dict:
    seeds = jax.random.split(jax.random.key(seed), 8)
    return {
        "latents": draw_latents(jax.random.fold_in(seeds[7], 71), 0),
        "shift_mod": scatter_about(seeds[1], (B, D), 0.5, 2.5, ((0, 4),)),
        "scale_mod": scatter_about(seeds[2], (B, D), 0.5, 2.5, ((0, 4),)),
        "gate_mod": jnp.clip(0.5 + 1.0 * jax.random.uniform(seeds[3], (B, D), jnp.float32) ** block_scale(seeds[3], (B, D), ((0, 4),), -0.2, 0.2), 0.5, 1.5).astype(jnp.bfloat16),
        "qkv_weight": draw_qkv_weight(jax.random.fold_in(seeds[7], 71), 0),
        "out_weight": scatter_about(seeds[5], (D, D), D ** -0.5, 0.1875),
        "cotangent": scatter_about(seeds[6], (B, F, P_SIZE, D), 1.0, 6.0, ((0, 4), (2, 32))),
    }


EPS = 1e-06

def norm_rows(values):
    floats = values.astype(jnp.float32)
    centre = lax.optimization_barrier(jnp.mean(floats, -1, keepdims=True))
    shifted = floats - centre
    variance = lax.optimization_barrier(jnp.mean(shifted * shifted, -1, keepdims=True))
    inverse = lax.rsqrt(variance + EPS)
    return (shifted * inverse, inverse)

def rounded(values):
    return lax.optimization_barrier(values.astype(jnp.bfloat16)).astype(jnp.float32)

def attend_forward(projected):
    parts = projected.reshape(P_SIZE, 3, H, HD).astype(jnp.float32)
    query, keys, values = (parts[:, 0], parts[:, 1], parts[:, 2])
    scores = jnp.einsum('qhd,khd->hqk', query, keys) / math.sqrt(HD)
    probs = jax.nn.softmax(scores, -1)
    mixed = jnp.einsum('hqk,khd->qhd', rounded(probs), values)
    return mixed.astype(jnp.bfloat16).reshape(P_SIZE, D)

def attend_backward(pair):
    projected, upstream = pair
    parts = projected.reshape(P_SIZE, 3, H, HD).astype(jnp.float32)
    query, keys, values = (parts[:, 0], parts[:, 1], parts[:, 2])
    grad = upstream.reshape(P_SIZE, H, HD).astype(jnp.float32)
    scores = jnp.einsum('qhd,khd->hqk', query, keys) / math.sqrt(HD)
    probs = jax.nn.softmax(scores, -1)
    value_grad = jnp.einsum('hqk,qhd->khd', rounded(probs), grad).astype(jnp.bfloat16)
    dprobs = jnp.einsum('qhd,khd->hqk', grad, values)
    total = lax.optimization_barrier(jnp.sum(probs * dprobs, -1, keepdims=True))
    score_grad = rounded(probs * (dprobs - total) / math.sqrt(HD))
    query_grad = jnp.einsum('hqk,khd->qhd', score_grad, keys).astype(jnp.bfloat16)
    key_grad = jnp.einsum('hqk,qhd->khd', score_grad, query).astype(jnp.bfloat16)
    return jnp.stack([query_grad, key_grad, value_grad], 1).reshape(P_SIZE, 3 * D)

def contract(left, right):
    return lax.dot_general(left, right, (((0,), (0,)), ((), ())), preferred_element_type=jnp.float32)

def reference(latents, shift_mod, scale_mod, gate_mod, qkv_weight, out_weight, cotangent):
    normed, inverse = norm_rows(latents)
    lift = 1.0 + scale_mod.astype(jnp.float32)[:, None, None, :]
    offset = shift_mod.astype(jnp.float32)[:, None, None, :]
    gating = gate_mod.astype(jnp.float32)[:, None, None, :]
    modulated = (normed * lift + offset).astype(jnp.bfloat16).reshape(-1, D)
    projected = jnp.dot(modulated, qkv_weight, preferred_element_type=jnp.float32).astype(jnp.bfloat16)
    items = projected.reshape(B * F, P_SIZE, 3 * D)
    attended = lax.map(attend_forward, items).reshape(-1, D)
    branch = jnp.dot(attended, out_weight, preferred_element_type=jnp.float32).reshape(B, F, P_SIZE, D)
    block_out = (latents.astype(jnp.float32) + gating * branch).astype(jnp.bfloat16)
    upstream = cotangent.astype(jnp.float32)
    branch_grad = (gating * upstream).astype(jnp.bfloat16).reshape(-1, D)
    attended_grad = lax.dot_general(branch_grad, out_weight, (((1,), (1,)), ((), ())), preferred_element_type=jnp.float32).astype(jnp.bfloat16)
    out_weight_grad = contract(attended, branch_grad)
    projected_grad = lax.map(attend_backward, (items, attended_grad.reshape(B * F, P_SIZE, D))).reshape(-1, 3 * D)
    qkv_weight_grad = contract(modulated, projected_grad)
    modulated_grad = lax.dot_general(projected_grad, qkv_weight, (((1,), (1,)), ((), ())), preferred_element_type=jnp.float32)
    normed_grad = modulated_grad.reshape(B, F, P_SIZE, D) * lift
    first = lax.optimization_barrier(jnp.mean(normed_grad, -1, keepdims=True))
    second = lax.optimization_barrier(jnp.mean(normed_grad * normed, -1, keepdims=True))
    latent_grad = (upstream + inverse * (normed_grad - first - normed * second)).astype(jnp.bfloat16)
    return (block_out, latent_grad, qkv_weight_grad, out_weight_grad)
```

```python
import functools
import math

import jax
import jax.numpy as jnp
from jax import lax
from jax.experimental import pallas as pl
from jax.experimental.pallas import tpu as pltpu
from jax.sharding import PartitionSpec as P

MESH = pl.DeviceIdType.MESH
F32 = jnp.float32
BF16 = jnp.bfloat16

D = 1152
HD = 72
HC = 8
HW = HC * HD
T = 512
PART = 768
EPS = 1e-06
SCALE = 1.0 / math.sqrt(HD)
LOG2E = math.log2(math.e)
VMEM_LIMIT = 56 * 1024 * 1024

VMEM_SPEC = pl.BlockSpec(memory_space=pltpu.VMEM)
ANY_SPEC = pl.BlockSpec(memory_space=pl.ANY)


def dot(a, b, ca=1, cb=0):
    return lax.dot_general(a, b, (((ca,), (cb,)), ((), ())), preferred_element_type=F32)


class Place:
    def __init__(self):
        self.dp = lax.axis_index("dp")
        self.seq = lax.axis_index("seq")
        self.z_lo = self.dp // 2
        self.core = self.dp % 2
        self.x = self.seq // 8
        self.z_hi = (self.seq // 4) % 2
        self.y = self.seq % 4
        self.z = self.z_hi * 2 + self.z_lo
        self.half = self.seq // 16
        self.frame = self.seq % 16

    def partner(self):
        return (self.z_lo * 2 + 1 - self.core, self.seq)

    def owner(self, j):
        return (self.z_lo * 2 + self.half, 16 * self.core + j)

    def owner_is_me(self, j):
        return jnp.logical_and(self.half == self.core, 16 * self.core + j == self.seq)

    def ring(self, axis, k):
        if axis == "x":
            p = (self.x + k) % 4
            return p, (self.dp, p * 8 + self.z_hi * 4 + self.y)
        if axis == "y":
            p = (self.y + k) % 4
            return p, (self.dp, self.x * 8 + self.z_hi * 4 + p)
        p = (self.z + k) % 4
        return p, ((p % 2) * 2 + self.core, self.x * 8 + (p // 2) * 4 + self.y)

    def at(self, axis):
        return {"x": self.x, "y": self.y, "z": self.z}[axis]


def remote(src, dst, send, recv, device):
    return pltpu.make_async_remote_copy(
        src_ref=src, dst_ref=dst, send_sem=send, recv_sem=recv, device_id=device, device_id_type=MESH
    )


def gather_kernel(lat, cot, mods, xs, cs, mods2, send, recv, fsend, msend, mrecv):
    me = Place()
    barrier = pltpu.get_barrier_semaphore()

    def greet(j, _):
        @pl.when(jnp.logical_not(me.owner_is_me(j)))
        def _():
            pl.semaphore_signal(barrier, inc=1, device_id=me.owner(j), device_id_type=MESH)

        return 0

    lax.fori_loop(0, 16, greet, 0)
    pl.semaphore_signal(barrier, inc=1, device_id=me.partner(), device_id_type=MESH)
    pl.semaphore_wait(barrier, 17 - jnp.where(me.half == me.core, 1, 0))

    mine = remote(mods, mods2.at[me.core], msend.at[0], mrecv.at[0], me.partner())
    mine.start()
    own = pltpu.make_async_copy(mods, mods2.at[me.core], msend.at[1])
    own.start()

    pairs = ((lat, xs), (cot, cs))
    for a, (src, dst) in enumerate(pairs):

        def put(j, _, a=a, src=src, dst=dst):
            @pl.when(me.owner_is_me(j))
            def _():
                pltpu.make_async_copy(src.at[j], dst.at[me.seq], recv.at[a, me.seq]).start()

            @pl.when(jnp.logical_not(me.owner_is_me(j)))
            def _():
                remote(src.at[j], dst.at[me.seq], send.at[a, j], recv.at[a, me.seq], me.owner(j)).start()

            return 0

        lax.fori_loop(0, 16, put, 0)

    for a, (src, dst) in enumerate(pairs):

        def forward(j, _, a=a, src=src, dst=dst):
            s = 16 * me.core + j

            @pl.when(me.owner_is_me(j))
            def _():
                pltpu.make_async_copy(src.at[j], dst.at[s], recv.at[a, s]).wait()

            @pl.when(jnp.logical_not(me.owner_is_me(j)))
            def _():
                remote(src.at[j], dst.at[s], send.at[a, j], recv.at[a, s], me.owner(j)).wait_recv()

            remote(dst.at[s], dst.at[s], fsend.at[a, j], recv.at[a, s], me.partner()).start()
            return 0

        lax.fori_loop(0, 16, forward, 0)

    for a, (src, dst) in enumerate(pairs):

        def finish(j, _, a=a, src=src, dst=dst):
            s = 16 * me.core + j
            o = 16 * (1 - me.core) + j
            remote(dst.at[s], dst.at[o], fsend.at[a, j], recv.at[a, o], me.partner()).wait_recv()
            remote(dst.at[s], dst.at[s], fsend.at[a, j], recv.at[a, s], me.partner()).wait_send()

            @pl.when(jnp.logical_not(me.owner_is_me(j)))
            def _():
                remote(src.at[j], dst.at[me.seq], send.at[a, j], recv.at[a, me.seq], me.owner(j)).wait_send()

            return 0

        lax.fori_loop(0, 16, finish, 0)
    mine.wait_send()
    remote(mods, mods2.at[1 - me.core], msend.at[0], mrecv.at[0], me.partner()).wait_recv()
    own.wait()


def gather_tokens(lat, cot, mods):
    tokens = jax.ShapeDtypeStruct((32, 16, D), BF16)
    return pl.pallas_call(
        gather_kernel,
        out_shape=(tokens, tokens, jax.ShapeDtypeStruct((2, 16, D), BF16)),
        in_specs=[ANY_SPEC] * 3,
        out_specs=(ANY_SPEC,) * 3,
        scratch_shapes=[
            pltpu.SemaphoreType.DMA((2, 16)),
            pltpu.SemaphoreType.DMA((2, 32)),
            pltpu.SemaphoreType.DMA((2, 16)),
            pltpu.SemaphoreType.DMA((2,)),
            pltpu.SemaphoreType.DMA((1,)),
        ],
        compiler_params=pltpu.CompilerParams(collective_id=0, has_side_effects=True),
    )(lat, cot, mods)


def norm_block(values):
    floats = values.astype(F32)
    shifted = floats - jnp.mean(floats, -1, keepdims=True)
    variance = jnp.mean(shifted * shifted, -1, keepdims=True)
    inverse = lax.rsqrt(variance + EPS)
    return shifted * inverse, inverse


def attend_kernel(x_ref, c_ref, mods_ref, wqkv_ref, wout_ref, m_ref, bg_ref, att_ref, pg_ref, mg_ref, head, grad):
    sel = lax.axis_index("seq") // 16
    mods = mods_ref[sel].astype(F32)
    shift = mods[0:1]
    lift = 1.0 + mods[1:2]
    gate = mods[2:3]
    rows = 128

    def project(i, _):
        at = pl.ds(pl.multiple_of(i * rows, rows), rows)
        normed, _ = norm_block(x_ref[at, :])
        modulated = (normed * lift + shift).astype(BF16)
        m_ref[at, :] = modulated
        branch = (gate * c_ref[at, :].astype(F32)).astype(BF16)
        bg_ref[at, :] = branch
        projected = dot(modulated, wqkv_ref[...]).astype(BF16)
        upstream = dot(branch, wout_ref[...], 1, 1).astype(BF16)
        for h in range(3 * HC):
            head[h, at, 0:HD] = projected[:, h * HD : (h + 1) * HD]
        for h in range(HC):
            head[3 * HC + h, at, 0:HD] = upstream[:, h * HD : (h + 1) * HD]
        return 0

    lax.fori_loop(0, T // rows, project, 0)

    cut = 256

    def one_head(h, _):
        keys = head[HC + h, :, 0:HD]
        values = head[2 * HC + h, :, 0:HD]
        key_grad = jnp.zeros((T, HD), F32)
        value_grad = jnp.zeros((T, HD), F32)
        for b in range(T // cut):
            at = pl.ds(b * cut, cut)
            query = head[h, at, 0:HD]
            up = head[3 * HC + h, at, 0:HD]
            scores = dot(keys, query, 1, 1)
            top = jnp.max(scores, 0, keepdims=True)
            weights = jnp.exp2((scores - top) * (SCALE * LOG2E))
            probs = weights * (1.0 / jnp.sum(weights, 0, keepdims=True))
            low = probs.astype(BF16)
            mixed = dot(values, low, 0, 0)
            grad[h, at, 0:HD] = mixed.T.astype(BF16)
            value_grad += dot(low, up)
            dprobs = dot(values, up, 1, 1)
            weighted = probs * dprobs
            total = jnp.sum(weighted, 0, keepdims=True)
            score_grad = ((weighted - probs * total) * SCALE).astype(BF16)
            key_grad += dot(score_grad, query)
            grad[HC + h, at, 0:HD] = dot(keys, score_grad, 0, 0).T.astype(BF16)
        grad[2 * HC + h, :, 0:HD] = key_grad.astype(BF16)
        grad[3 * HC + h, :, 0:HD] = value_grad.astype(BF16)
        return 0

    lax.fori_loop(0, HC, one_head, 0)

    def merge(i, _):
        at = pl.ds(pl.multiple_of(i * rows, rows), rows)
        att_ref[at, :] = jnp.concatenate([grad[h, at, 0:HD] for h in range(HC)], 1)
        joined = jnp.concatenate([grad[HC + h, at, 0:HD] for h in range(3 * HC)], 1)
        pg_ref[at, :] = joined
        mg_ref[at, :] = dot(joined, wqkv_ref[...], 1, 1)
        return 0

    lax.fori_loop(0, T // rows, merge, 0)


def attend(x, c, mods2, wqkv, wout):
    return pl.pallas_call(
        attend_kernel,
        out_shape=(
            jax.ShapeDtypeStruct((T, D), BF16),
            jax.ShapeDtypeStruct((T, D), BF16),
            jax.ShapeDtypeStruct((T, HW), BF16),
            jax.ShapeDtypeStruct((T, 3 * HW), BF16),
            jax.ShapeDtypeStruct((T, D), F32),
        ),
        in_specs=[VMEM_SPEC] * 5,
        out_specs=(VMEM_SPEC,) * 5,
        scratch_shapes=[pltpu.VMEM((4 * HC, T, 128), BF16), pltpu.VMEM((4 * HC, T, 128), BF16)],
        compiler_params=pltpu.CompilerParams(vmem_limit_bytes=VMEM_LIMIT),
    )(x, c, mods2, wqkv, wout)


ORDERS = (("x", "y", "z"), ("y", "z", "x"), ("z", "x", "y"))


def natural_row(order, p):
    chunk = (p * 7282) >> 16
    inner = p - chunk * 9
    core = chunk & 1
    digits = {order[2]: (chunk >> 1) & 3, order[1]: (chunk >> 3) & 3, order[0]: chunk >> 5}
    z = digits["z"]
    block = (z & 1) * 64 + core * 32 + digits["x"] * 8 + (z >> 1) * 4 + digits["y"]
    return block * 9 + inner


def pick_rows(order, first, count):
    place = first + lax.broadcasted_iota(jnp.int32, (count, 1), 0)
    row = natural_row(order, place)
    column = lax.broadcasted_iota(jnp.int32, (count, D), 1)
    return jnp.where(row == column, 1.0, 0.0).astype(BF16)


def reduce_kernel(
    x_ref, c_ref, mods_ref, m_ref, bg_ref, att_ref, pg_ref, mg_ref, wout_ref,
    bo_ref, lg_ref, qkvg_ref, outg_ref,
    att_other, att_all, mg_other, bo_s, lg_s, bg_half, g1, r1, g2, r2, g3, r3, f4, r4,
    psend, precv, osend, orecv, s1, v1, s2, v2, s3, v3, s4, v4,
):
    me = Place()
    barrier = pltpu.get_barrier_semaphore()

    def greet(j, _):
        @pl.when(jnp.logical_not(me.owner_is_me(j)))
        def _():
            pl.semaphore_signal(barrier, inc=1, device_id=me.owner(j), device_id_type=MESH)

        return 0

    lax.fori_loop(0, 16, greet, 0)
    for axis in "xyz":
        for k in range(1, 4):
            pl.semaphore_signal(barrier, inc=1, device_id=me.ring(axis, k)[1], device_id_type=MESH)
    pl.semaphore_signal(barrier, inc=1, device_id=me.partner(), device_id_type=MESH)
    pl.semaphore_wait(barrier, 26 - jnp.where(me.half == me.core, 1, 0))

    other_rows = pl.ds(pl.multiple_of((1 - me.core) * 256, 256), 256)
    my_rows = pl.ds(pl.multiple_of(me.core * 256, 256), 256)
    swap_att = remote(att_ref, att_other, psend.at[0], precv.at[0], me.partner())
    swap_att.start()
    swap_mg = remote(mg_ref.at[other_rows], mg_other, psend.at[1], precv.at[1], me.partner())
    swap_mg.start()

    first = me.core == 0

    def ring_send(part, axis, k, src, dst, send, recv):
        p, device = me.ring(axis, k)
        return remote(src.at[part, p], dst.at[part, k - 1], send.at[part, k - 1], recv.at[part, k - 1], device)

    def products(part):
        order = ORDERS[part]
        for k in (1, 2, 3, 0):
            p, _ = me.ring(order[0], k)
            choose = pick_rows(order, p * 288, 288)
            left = dot(choose, m_ref[...], 1, 1).astype(BF16)
            if part < 2:
                block = dot(left, pg_ref[:, part * PART : (part + 1) * PART])
                g1[part, p] = block.astype(BF16)
            else:
                block = dot(left, pg_ref[:, 2 * PART : 3 * HW])
                a_left = dot(choose, att_all[...], 1, 1).astype(BF16)
                tail = dot(a_left, bg_half[...])
                g1[part, p] = jnp.concatenate([block, tail], 1).astype(BF16)
            if k > 0:
                ring_send(part, order[0], k, g1, r1, s1, v1).start()

    products(0)
    products(1)
    swap_att.wait()
    mine, theirs = att_ref[...], att_other[...]
    att_all[:, 0:HW] = jnp.where(first, mine, theirs)
    att_all[:, HW:] = jnp.where(first, theirs, mine)
    bg_half[...] = jnp.where(first, bg_ref[:, 0:HW], bg_ref[:, HW:])
    products(2)

    sel = me.half
    mods = mods_ref[sel].astype(F32)
    lift = 1.0 + mods[1:2]
    gate = mods[2:3]
    tokens = x_ref[my_rows, :]
    branch = dot(att_all[my_rows, :], wout_ref[...])
    out = (tokens.astype(F32) + gate * branch).astype(BF16)
    bo_s[...] = out.reshape(16, 16, D)

    def back(a, staged, out_ref):
        def put(j, _):
            @pl.when(me.owner_is_me(j))
            def _():
                pltpu.make_async_copy(staged.at[j], out_ref.at[me.frame], orecv.at[a, me.frame]).start()

            @pl.when(jnp.logical_not(me.owner_is_me(j)))
            def _():
                remote(staged.at[j], out_ref.at[me.frame], osend.at[a, j], orecv.at[a, me.frame], me.owner(j)).start()

            return 0

        lax.fori_loop(0, 16, put, 0)

    back(0, bo_s, bo_ref)
    swap_mg.wait()
    normed, inverse = norm_block(tokens)
    normed_grad = (mg_ref[my_rows, :] + mg_other[...]) * lift
    mean = jnp.mean(normed_grad, -1, keepdims=True)
    second = jnp.mean(normed_grad * normed, -1, keepdims=True)
    latent = c_ref[my_rows, :].astype(F32) + inverse * (normed_grad - mean - normed * second)
    lg_s[...] = latent.astype(BF16).reshape(16, 16, D)
    back(1, lg_s, lg_ref)

    for part in range(3):
        a, b, c = ORDERS[part]
        for k in range(1, 4):
            ring_send(part, a, k, g1, r1, s1, v1).wait_recv()
        total = g1[part, me.at(a)].astype(F32)
        for k in range(3):
            total += r1[part, k].astype(F32)
        for p in range(4):
            g2[part, p, 0:72] = total[p * 72 : (p + 1) * 72].astype(BF16)
            g2[part, p, 72:80] = jnp.zeros((8, PART), BF16)
        for k in range(1, 4):
            ring_send(part, b, k, g2, r2, s2, v2).start()
    for part in range(3):
        a, b, c = ORDERS[part]
        for k in range(1, 4):
            ring_send(part, b, k, g2, r2, s2, v2).wait_recv()
        total = g2[part, me.at(b)].astype(F32)
        for k in range(3):
            total += r2[part, k].astype(F32)
        for p in range(4):
            for core in range(2):
                at = p * 18 + core * 9
                g3[part, p, core * 16 : core * 16 + 16] = jnp.concatenate(
                    [total[at : at + 9], jnp.zeros((7, PART), F32)], 0
                ).astype(BF16)
        for k in range(1, 4):
            ring_send(part, c, k, g3, r3, s3, v3).start()
    for part in range(3):
        a, b, c = ORDERS[part]
        for k in range(1, 4):
            ring_send(part, c, k, g3, r3, s3, v3).wait_recv()
        total = g3[part, me.at(c)].astype(F32)
        for k in range(3):
            total += r3[part, k].astype(F32)
        f4[part] = total.reshape(2, 16, PART)
        remote(f4.at[part, 1 - me.core], r4.at[part], s4.at[part], v4.at[part], me.partner()).start()
    for part in range(3):
        remote(f4.at[part, 1 - me.core], r4.at[part], s4.at[part], v4.at[part], me.partner()).wait_recv()
    mine = jnp.concatenate([f4[part, me.core] for part in range(3)], 1)
    theirs = jnp.concatenate([r4[part] for part in range(3)], 1)
    low = jnp.where(first, mine, theirs)[0:9]
    high = jnp.where(first, theirs, mine)[0:9]
    for i in range(3):
        qkvg_ref[:, i * D : i * D + HW] = low[:, i * HW : (i + 1) * HW]
        qkvg_ref[:, i * D + HW : (i + 1) * D] = high[:, i * HW : (i + 1) * HW]
    outg_ref[:, 0:HW] = low[:, 3 * HW :]
    outg_ref[:, HW:] = high[:, 3 * HW :]

    for part in range(3):
        a, b, c = ORDERS[part]
        for k in range(1, 4):
            ring_send(part, a, k, g1, r1, s1, v1).wait_send()
            ring_send(part, b, k, g2, r2, s2, v2).wait_send()
            ring_send(part, c, k, g3, r3, s3, v3).wait_send()
        remote(f4.at[part, 1 - me.core], r4.at[part], s4.at[part], v4.at[part], me.partner()).wait_send()

    for a, (staged, out_ref) in enumerate(((bo_s, bo_ref), (lg_s, lg_ref))):

        def finish(j, _, a=a, staged=staged, out_ref=out_ref):
            @pl.when(me.owner_is_me(j))
            def _():
                pltpu.make_async_copy(staged.at[j], out_ref.at[j], orecv.at[a, j]).wait()

            @pl.when(jnp.logical_not(me.owner_is_me(j)))
            def _():
                copy = remote(staged.at[j], out_ref.at[j], osend.at[a, j], orecv.at[a, j], me.owner(j))
                copy.wait_recv()
                copy.wait_send()

            return 0

        lax.fori_loop(0, 16, finish, 0)


def reduce_all(*operands):
    dma = pltpu.SemaphoreType.DMA
    return pl.pallas_call(
        reduce_kernel,
        out_shape=(
            jax.ShapeDtypeStruct((16, 16, D), BF16),
            jax.ShapeDtypeStruct((16, 16, D), BF16),
            jax.ShapeDtypeStruct((9, 3 * D), F32),
            jax.ShapeDtypeStruct((9, D), F32),
        ),
        in_specs=[VMEM_SPEC] * 9,
        out_specs=(ANY_SPEC, ANY_SPEC, VMEM_SPEC, VMEM_SPEC),
        scratch_shapes=[
            pltpu.VMEM((T, HW), BF16),
            pltpu.VMEM((T, D), BF16),
            pltpu.VMEM((T // 2, D), F32),
            pltpu.VMEM((16, 16, D), BF16),
            pltpu.VMEM((16, 16, D), BF16),
            pltpu.VMEM((T, HW), BF16),
            pltpu.VMEM((3, 4, 288, PART), BF16),
            pltpu.VMEM((3, 3, 288, PART), BF16),
            pltpu.VMEM((3, 4, 80, PART), BF16),
            pltpu.VMEM((3, 3, 80, PART), BF16),
            pltpu.VMEM((3, 4, 32, PART), BF16),
            pltpu.VMEM((3, 3, 32, PART), BF16),
            pltpu.VMEM((3, 2, 16, PART), F32),
            pltpu.VMEM((3, 16, PART), F32),
            dma((2,)),
            dma((2,)),
            dma((2, 16)),
            dma((2, 16)),
            dma((3, 3)),
            dma((3, 3)),
            dma((3, 3)),
            dma((3, 3)),
            dma((3, 3)),
            dma((3, 3)),
            dma((3,)),
            dma((3,)),
        ],
        compiler_params=pltpu.CompilerParams(
            collective_id=1, has_side_effects=True, vmem_limit_bytes=VMEM_LIMIT
        ),
    )(*operands)


def on_device(latents, shift_mod, scale_mod, gate_mod, qkv_weight, out_weight, cotangent):
    core = lax.axis_index("dp") % 2
    mods = jnp.concatenate([shift_mod, scale_mod, gate_mod, jnp.zeros((13, D), BF16)], 0)
    wqkv = lax.dynamic_slice_in_dim(qkv_weight.reshape(D, 3, 2, HW), core, 1, 2).reshape(D, 3 * HW)
    wout = lax.dynamic_slice_in_dim(out_weight, core * HW, HW, 0)
    x, c, mods2 = gather_tokens(latents[0], cotangent[0], mods)
    x = x.reshape(T, D)
    c = c.reshape(T, D)
    m, bg, att, pg, mg = attend(x, c, mods2, wqkv, wout)
    bo, lg, qkvg, outg = reduce_all(x, c, mods2, m, bg, att, pg, mg, out_weight)
    return bo[None], lg[None], qkvg, outg


def solution(mesh):
    in_specs = (
        P("dp", None, "seq", None),
        P("dp", None),
        P("dp", None),
        P("dp", None),
        P(),
        P(),
        P("dp", None, "seq", None),
    )
    out_specs = (
        P("dp", None, "seq", None),
        P("dp", None, "seq", None),
        P(("dp", "seq"), None),
        P(("dp", "seq"), None),
    )
    return jax.shard_map(
        on_device, mesh=mesh, in_specs=in_specs, out_specs=out_specs, check_vma=False
    )
```

```python
import math

import jax
import jax.numpy as jnp
from jax import lax
from jax.experimental import pallas as pl
from jax.experimental.pallas import tpu as pltpu
from jax.sharding import PartitionSpec as P

MESH = pl.DeviceIdType.MESH
F32 = jnp.float32
BF16 = jnp.bfloat16

D = 1152
HD = 72
HC = 8
HW = HC * HD
T = 512
EPS = 1e-06
SCALE = 1.0 / math.sqrt(HD)
LOG2E = math.log2(math.e)
VMEM_LIMIT = 60 * 1024 * 1024
ROWS = 128
CUT = 256

ORDERS = (("x", "y", "z"), ("y", "z", "x"), ("z", "x", "y"))

VMEM_SPEC = pl.BlockSpec(memory_space=pltpu.VMEM)
ANY_SPEC = pl.BlockSpec(memory_space=pl.ANY)


def dot(a, b, ca=1, cb=0):
    return lax.dot_general(a, b, (((ca,), (cb,)), ((), ())), preferred_element_type=F32)


class Place:
    def __init__(self):
        self.dp = lax.axis_index("dp")
        self.seq = lax.axis_index("seq")
        self.z_lo = self.dp // 2
        self.core = self.dp % 2
        self.x = self.seq // 8
        self.z_hi = (self.seq // 4) % 2
        self.y = self.seq % 4
        self.z = self.z_hi * 2 + self.z_lo
        self.half = self.seq // 16
        self.frame = self.seq % 16

    def partner(self):
        return (self.z_lo * 2 + 1 - self.core, self.seq)

    def owner(self, j):
        return (self.z_lo * 2 + self.half, 16 * self.core + j)

    def owner_is_me(self, j):
        return jnp.logical_and(self.half == self.core, 16 * self.core + j == self.seq)

    def ring(self, axis, k):
        if axis == "x":
            p = (self.x + k) % 4
            return p, (self.dp, p * 8 + self.z_hi * 4 + self.y)
        if axis == "y":
            p = (self.y + k) % 4
            return p, (self.dp, self.x * 8 + self.z_hi * 4 + p)
        p = (self.z + k) % 4
        return p, ((p % 2) * 2 + self.core, self.x * 8 + (p // 2) * 4 + self.y)

    def at(self, axis):
        return {"x": self.x, "y": self.y, "z": self.z}[axis]


def remote(src, dst, send, recv, device):
    return pltpu.make_async_remote_copy(
        src_ref=src, dst_ref=dst, send_sem=send, recv_sem=recv, device_id=device, device_id_type=MESH
    )


def norm_block(values):
    floats = values.astype(F32)
    shifted = floats - jnp.mean(floats, -1, keepdims=True)
    variance = jnp.mean(shifted * shifted, -1, keepdims=True)
    inverse = lax.rsqrt(variance + EPS)
    return shifted * inverse, inverse


def pick_rows(part):
    order = ORDERS[part]
    p = lax.broadcasted_iota(jnp.int32, (384, 1), 0)
    chunk = (p * 10923) >> 16
    inner = p - chunk * 6 + part * 6
    digits = {order[2]: chunk & 3, order[1]: (chunk >> 2) & 3, order[0]: chunk >> 4}
    z = digits["z"]
    core = jnp.where(inner >= 9, 1, 0)
    block = (z & 1) * 64 + core * 32 + digits["x"] * 8 + (z >> 1) * 4 + digits["y"]
    row = block * 9 + inner - core * 9
    column = lax.broadcasted_iota(jnp.int32, (384, D), 1)
    return jnp.where(row == column, 1.0, 0.0).astype(BF16)


def block_kernel(
    lat, cot, shift_ref, scale_ref, gate_ref, wqkv_hbm, wout_hbm,
    bo_ref, lg_ref, qkvg_ref, outg_ref,
    xs, cs, mods, wfull, wqkv, wout, pick, m, mt, bg, bg_half, head, probs_s, att, att_other, at_t, grad, pg,
    mg, mg_other, bo_s, lg_s, g1, r1, g2, r2, g3, r3, f4, r4,
    send, recv, fsend, msem, wsem, psend, precv, osend, orecv, s1, v1, s2, v2, s3, v3, s4, v4,
):
    me = Place()
    first = me.core == 0

    weights = [pltpu.make_async_copy(wout_hbm, wout, wsem.at[3])]
    for i in range(3):
        columns = pl.ds(pl.multiple_of(i * D + me.core * 512, 128), 640)
        weights.append(pltpu.make_async_copy(wqkv_hbm.at[:, columns], wfull.at[i], wsem.at[i]))
    for copy in weights:
        copy.start()

    barrier = pltpu.get_barrier_semaphore()

    def greet(j, _):
        @pl.when(jnp.logical_not(me.owner_is_me(j)))
        def _():
            pl.semaphore_signal(barrier, inc=1, device_id=me.owner(j), device_id_type=MESH)

        return 0

    lax.fori_loop(0, 16, greet, 0)
    for axis in "xyz":
        for k in range(1, 4):
            pl.semaphore_signal(barrier, inc=1, device_id=me.ring(axis, k)[1], device_id_type=MESH)
    pl.semaphore_signal(barrier, inc=1, device_id=me.partner(), device_id_type=MESH)
    mods[me.core, 0:1] = shift_ref[...].astype(F32)
    mods[me.core, 1:2] = 1.0 + scale_ref[...].astype(F32)
    mods[me.core, 2:3] = gate_ref[...].astype(F32)
    mods[me.core, 3:8] = jnp.zeros((5, D), F32)
    pl.semaphore_wait(barrier, 26 - jnp.where(me.half == me.core, 1, 0))

    pairs = ((lat, xs), (cot, cs))
    for a, (src, dst) in enumerate(pairs):

        def put(t, _, a=a, src=src, dst=dst):
            j = (t + me.seq) % 16

            @pl.when(me.owner_is_me(j))
            def _():
                pltpu.make_async_copy(src.at[j], dst.at[me.seq], recv.at[a, me.seq]).start()

            @pl.when(jnp.logical_not(me.owner_is_me(j)))
            def _():
                remote(src.at[j], dst.at[me.seq], send.at[a, j], recv.at[a, me.seq], me.owner(j)).start()

            return 0

        lax.fori_loop(0, 16, put, 0)
    swap_mods = remote(mods.at[me.core], mods.at[me.core], msem.at[0], msem.at[1], me.partner())
    swap_mods.start()

    for part in range(3):
        pick[part * 384 : (part + 1) * 384] = pick_rows(part)
    for copy in weights:
        copy.wait()

    @pl.when(first)
    def _():
        for i in range(3):
            wqkv[:, i * HW : (i + 1) * HW] = wfull[i, :, 0:HW]

    @pl.when(jnp.logical_not(first))
    def _():
        for i in range(3):
            wqkv[:, i * HW : (i + 1) * HW] = wfull[i, :, 64:640]

    def share(a):
        src, dst = pairs[a]

        def forward(t, _):
            j = (me.frame - t) % 16
            s = 16 * me.core + j

            @pl.when(me.owner_is_me(j))
            def _():
                pltpu.make_async_copy(src.at[j], dst.at[s], recv.at[a, s]).wait()

            @pl.when(jnp.logical_not(me.owner_is_me(j)))
            def _():
                remote(src.at[j], dst.at[s], send.at[a, j], recv.at[a, s], me.owner(j)).wait_recv()

            remote(dst.at[s], dst.at[s], fsend.at[a, j], recv.at[a, s], me.partner()).start()
            return 0

        lax.fori_loop(0, 16, forward, 0)

        def arrive(j, _):
            s = 16 * me.core + j
            o = 16 * (1 - me.core) + j
            remote(dst.at[s], dst.at[o], fsend.at[a, j], recv.at[a, o], me.partner()).wait_recv()
            return 0

        lax.fori_loop(0, 16, arrive, 0)

    share(0)
    remote(mods.at[me.core], mods.at[1 - me.core], msem.at[0], msem.at[1], me.partner()).wait_recv()
    shift = mods[me.half, 0:1]
    lift = mods[me.half, 1:2]
    gate = mods[me.half, 2:3]

    def project(i, _):
        at = pl.ds(pl.multiple_of(i * ROWS, ROWS), ROWS)
        normed, _ = norm_block(xs[pl.ds(i * (ROWS // 16), ROWS // 16)].reshape(ROWS, D))
        modulated = (normed * lift + shift).astype(BF16)
        m[at, :] = modulated
        projected = dot(modulated, wqkv[...]).astype(BF16)
        for h in range(3 * HC):
            head[h, at, 0:HD] = projected[:, h * HD : (h + 1) * HD]
        return 0

    lax.fori_loop(0, T // ROWS, project, 0)

    def turn(part, _):
        at = pl.ds(pl.multiple_of(part * 384, 384), 384)
        mt[at, :] = dot(pick[at, :], m[...], 1, 1).astype(BF16)
        return 0

    lax.fori_loop(0, 3, turn, 0)
    share(1)

    def upstream(i, _):
        at = pl.ds(pl.multiple_of(i * ROWS, ROWS), ROWS)
        cotangent = cs[pl.ds(i * (ROWS // 16), ROWS // 16)].reshape(ROWS, D).astype(F32)
        branch = (gate * cotangent).astype(BF16)
        bg[at, :] = branch
        my_wout = wout[pl.ds(pl.multiple_of(me.core * HW, HW), HW), :]
        up = dot(branch, my_wout, 1, 1).astype(BF16)
        for h in range(HC):
            head[3 * HC + h, at, 0:HD] = up[:, h * HD : (h + 1) * HD]
        return 0

    lax.fori_loop(0, T // ROWS, upstream, 0)

    def forward_head(h, _):
        keys = head[HC + h, :, 0:HD]
        values = head[2 * HC + h, :, 0:HD]
        value_grad = jnp.zeros((T, HD), F32)
        for b in range(T // CUT):
            at = pl.ds(b * CUT, CUT)
            scores = dot(keys, head[h, at, 0:HD], 1, 1)
            top = jnp.max(scores, 0, keepdims=True)
            weights = jnp.exp2((scores - top) * (SCALE * LOG2E))
            probs = weights * (1.0 / jnp.sum(weights, 0, keepdims=True))
            probs_s[h, b] = probs
            low = probs.astype(BF16)
            grad[3 * HC + h, at, 0:HD] = dot(values, low, 0, 0).T.astype(BF16)
            value_grad += dot(low, head[3 * HC + h, at, 0:HD])
        grad[2 * HC + h, :, 0:HD] = value_grad.astype(BF16)
        return 0

    lax.fori_loop(0, HC, forward_head, 0)

    def join(first_head, target, column):
        def rows(i, _):
            at = pl.ds(pl.multiple_of(i * ROWS, ROWS), ROWS)
            target[at, column : column + HW] = jnp.concatenate(
                [grad[first_head + h, at, 0:HD] for h in range(HC)], 1
            )
            return 0

        lax.fori_loop(0, T // ROWS, rows, 0)

    join(3 * HC, att, 0)
    swap_att = remote(att, att_other, psend.at[0], precv.at[0], me.partner())
    swap_att.start()
    join(2 * HC, pg, 2 * HW)

    def ring_copy(chunk, part, axis, k, src, dst, send, recv):
        p, device = me.ring(axis, k)
        return remote(
            src.at[chunk, part, p],
            dst.at[chunk, part, k - 1],
            send.at[chunk, part, k - 1],
            recv.at[chunk, part, k - 1],
            device,
        )

    def stage_one(chunk, part, block):
        for p in range(4):
            g1[chunk, part, p] = block[p * 96 : (p + 1) * 96]
        for k in (2, 1, 3):
            ring_copy(chunk, part, ORDERS[part][0], k, g1, r1, s1, v1).start()

    def stage_two(chunk):
        for part in range(3):
            a, b, _ = ORDERS[part]
            for k in range(1, 4):
                ring_copy(chunk, part, a, k, g1, r1, s1, v1).wait_recv()
            total = g1[chunk, part, me.at(a)].astype(F32)
            for k in range(3):
                total += r1[chunk, part, k].astype(F32)
            for p in range(4):
                g2[chunk, part, p] = jnp.concatenate(
                    [total[p * 24 : (p + 1) * 24], jnp.zeros((8, D), F32)], 0
                ).astype(BF16)
            for k in (2, 1, 3):
                ring_copy(chunk, part, b, k, g2, r2, s2, v2).start()

    def stage_three(chunk):
        for part in range(3):
            _, b, c = ORDERS[part]
            for k in range(1, 4):
                ring_copy(chunk, part, b, k, g2, r2, s2, v2).wait_recv()
            total = g2[chunk, part, me.at(b)].astype(F32)
            for k in range(3):
                total += r2[chunk, part, k].astype(F32)
            for p in range(4):
                g3[chunk, part, p] = jnp.concatenate(
                    [total[p * 6 : (p + 1) * 6], jnp.zeros((10, D), F32)], 0
                ).astype(BF16)
            for k in (2, 1, 3):
                ring_copy(chunk, part, c, k, g3, r3, s3, v3).start()

    def swap_rows(chunk):
        return remote(f4.at[chunk, 1 - me.core], r4.at[chunk], s4.at[chunk], v4.at[chunk], me.partner())

    def stage_four(chunk):
        rows = []
        for part in range(3):
            _, _, c = ORDERS[part]
            for k in range(1, 4):
                ring_copy(chunk, part, c, k, g3, r3, s3, v3).wait_recv()
            total = g3[chunk, part, me.at(c)].astype(F32)
            for k in range(3):
                total += r3[chunk, part, k].astype(F32)
            rows.append(total[0:6])
        rows = jnp.concatenate(rows, 0)
        pad = jnp.zeros((7, D), F32)
        f4[chunk, 0] = jnp.concatenate([rows[0:9], pad], 0)
        f4[chunk, 1] = jnp.concatenate([rows[9:18], pad], 0)
        swap_rows(chunk).start()

    def stage_five(chunk):
        swap_rows(chunk).wait_recv()
        mine, theirs = f4[chunk, me.core], r4[chunk]
        return jnp.where(first, mine, theirs)[0:9], jnp.where(first, theirs, mine)[0:9]

    swap_att.wait()
    att_all = m
    mine, theirs = att[...], att_other[...]
    att_all[:, 0:HW] = jnp.where(first, mine, theirs)
    att_all[:, HW:] = jnp.where(first, theirs, mine)
    bg_half[...] = jnp.where(first, bg[:, 0:HW], bg[:, HW:])
    for part in range(3):
        at = pl.ds(part * 384, 384)
        at_t[at, :] = dot(pick[at, :], att_all[...], 1, 1).astype(BF16)
        value_part = dot(mt[at, :], pg[:, 2 * HW :])
        out_part = dot(at_t[at, :], bg_half[...])
        stage_one(0, part, jnp.concatenate([value_part, out_part], 1).astype(BF16))

    def back(a, staged, out_ref):
        def put(t, _):
            j = (me.frame - t) % 16

            @pl.when(me.owner_is_me(j))
            def _():
                pltpu.make_async_copy(staged.at[j], out_ref.at[me.frame], orecv.at[a, me.frame]).start()

            @pl.when(jnp.logical_not(me.owner_is_me(j)))
            def _():
                remote(staged.at[j], out_ref.at[me.frame], osend.at[a, j], orecv.at[a, me.frame], me.owner(j)).start()

            return 0

        lax.fori_loop(0, 16, put, 0)

    def finish_block(i, _):
        at = pl.ds(pl.multiple_of(me.core * 256 + i * ROWS, ROWS), ROWS)
        tiles = pl.ds(me.core * 16 + i * (ROWS // 16), ROWS // 16)
        branch = dot(att_all[at, :], wout[...])
        out = (xs[tiles].reshape(ROWS, D).astype(F32) + gate * branch).astype(BF16)
        bo_s[pl.ds(i * (ROWS // 16), ROWS // 16)] = out.reshape(ROWS // 16, 16, D)
        return 0

    lax.fori_loop(0, 256 // ROWS, finish_block, 0)
    back(0, bo_s, bo_ref)

    def backward_head(h, _):
        keys = head[HC + h, :, 0:HD]
        values = head[2 * HC + h, :, 0:HD]
        key_grad = jnp.zeros((T, HD), F32)
        for b in range(T // CUT):
            at = pl.ds(b * CUT, CUT)
            query = head[h, at, 0:HD]
            dprobs = dot(values, head[3 * HC + h, at, 0:HD], 1, 1)
            probs = probs_s[h, b]
            weighted = probs * dprobs
            total = jnp.sum(weighted, 0, keepdims=True)
            score_grad = ((weighted - probs * total) * SCALE).astype(BF16)
            key_grad += dot(score_grad, query)
            grad[h, at, 0:HD] = dot(keys, score_grad, 0, 0).T.astype(BF16)
        grad[HC + h, :, 0:HD] = key_grad.astype(BF16)
        return 0

    lax.fori_loop(0, 4, backward_head, 0)
    stage_two(0)
    lax.fori_loop(4, 6, backward_head, 0)
    stage_three(0)
    lax.fori_loop(6, 8, backward_head, 0)
    stage_four(0)
    join(0, pg, 0)
    join(HC, pg, HW)

    for part in range(3):
        at = pl.ds(part * 384, 384)
        stage_one(1, part, dot(mt[at, :], pg[:, 0 : 2 * HW]).astype(BF16))

    def modulated_grad(i, _):
        at = pl.ds(pl.multiple_of((1 - me.core) * 256 + i * ROWS, ROWS), ROWS)
        mg[pl.ds(pl.multiple_of(i * ROWS, ROWS), ROWS), :] = dot(pg[at, :], wqkv[...], 1, 1)
        return 0

    lax.fori_loop(0, 256 // ROWS, modulated_grad, 0)
    swap_mg = remote(mg, mg_other, psend.at[1], precv.at[1], me.partner())
    swap_mg.start()
    own_grad = dot(pg[pl.ds(pl.multiple_of(me.core * 256, 256), 256), :], wqkv[...], 1, 1)
    swap_mg.wait()
    for i in range(256 // ROWS):
        tiles = pl.ds(me.core * 16 + i * (ROWS // 16), ROWS // 16)
        normed, inverse = norm_block(xs[tiles].reshape(ROWS, D))
        normed_grad = (own_grad[i * ROWS : (i + 1) * ROWS] + mg_other[i * ROWS : (i + 1) * ROWS, :]) * lift
        mean = jnp.mean(normed_grad, -1, keepdims=True)
        second = jnp.mean(normed_grad * normed, -1, keepdims=True)
        latent = cs[tiles].reshape(ROWS, D).astype(F32) + inverse * (normed_grad - mean - normed * second)
        lg_s[i * (ROWS // 16) : (i + 1) * (ROWS // 16)] = latent.astype(BF16).reshape(ROWS // 16, 16, D)
    back(1, lg_s, lg_ref)

    stage_two(1)
    low, high = stage_five(0)
    qkvg_ref[:, 2 * D : 2 * D + HW] = low[:, 0:HW]
    qkvg_ref[:, 2 * D + HW : 3 * D] = high[:, 0:HW]
    outg_ref[:, 0:HW] = low[:, HW:]
    outg_ref[:, HW:] = high[:, HW:]
    stage_three(1)
    stage_four(1)
    low, high = stage_five(1)
    for i in range(2):
        qkvg_ref[:, i * D : i * D + HW] = low[:, i * HW : (i + 1) * HW]
        qkvg_ref[:, i * D + HW : (i + 1) * D] = high[:, i * HW : (i + 1) * HW]

    for chunk in range(2):
        for part in range(3):
            a, b, c = ORDERS[part]
            for k in range(1, 4):
                ring_copy(chunk, part, a, k, g1, r1, s1, v1).wait_send()
                ring_copy(chunk, part, b, k, g2, r2, s2, v2).wait_send()
                ring_copy(chunk, part, c, k, g3, r3, s3, v3).wait_send()
        swap_rows(chunk).wait_send()
    swap_mods.wait_send()
    for a, (src, dst) in enumerate(pairs):

        def sent(j, _, a=a, src=src, dst=dst):
            s = 16 * me.core + j
            remote(dst.at[s], dst.at[s], fsend.at[a, j], recv.at[a, s], me.partner()).wait_send()

            @pl.when(jnp.logical_not(me.owner_is_me(j)))
            def _():
                remote(src.at[j], dst.at[me.seq], send.at[a, j], recv.at[a, me.seq], me.owner(j)).wait_send()

            return 0

        lax.fori_loop(0, 16, sent, 0)
    for a, (staged, out_ref) in enumerate(((bo_s, bo_ref), (lg_s, lg_ref))):

        def finish(j, _, a=a, staged=staged, out_ref=out_ref):
            @pl.when(me.owner_is_me(j))
            def _():
                pltpu.make_async_copy(staged.at[j], out_ref.at[j], orecv.at[a, j]).wait()

            @pl.when(jnp.logical_not(me.owner_is_me(j)))
            def _():
                copy = remote(staged.at[j], out_ref.at[j], osend.at[a, j], orecv.at[a, j], me.owner(j))
                copy.wait_recv()
                copy.wait_send()

            return 0

        lax.fori_loop(0, 16, finish, 0)


def run_block(*operands):
    dma = pltpu.SemaphoreType.DMA
    vmem = pltpu.VMEM
    return pl.pallas_call(
        block_kernel,
        out_shape=(
            jax.ShapeDtypeStruct((16, 16, D), BF16),
            jax.ShapeDtypeStruct((16, 16, D), BF16),
            jax.ShapeDtypeStruct((9, 3 * D), F32),
            jax.ShapeDtypeStruct((9, D), F32),
        ),
        in_specs=[ANY_SPEC, ANY_SPEC, VMEM_SPEC, VMEM_SPEC, VMEM_SPEC, ANY_SPEC, ANY_SPEC],
        out_specs=(ANY_SPEC, ANY_SPEC, VMEM_SPEC, VMEM_SPEC),
        scratch_shapes=[
            vmem((32, 16, D), BF16),
            vmem((32, 16, D), BF16),
            vmem((2, 8, D), F32),
            vmem((3, D, 640), BF16),
            vmem((D, 3 * HW), BF16),
            vmem((D, D), BF16),
            vmem((D, D), BF16),
            vmem((T, D), BF16),
            vmem((D, T), BF16),
            vmem((T, D), BF16),
            vmem((T, HW), BF16),
            vmem((4 * HC, T, 128), BF16),
            vmem((HC, T // CUT, T, CUT), F32),
            vmem((T, HW), BF16),
            vmem((T, HW), BF16),
            vmem((D, T), BF16),
            vmem((4 * HC, T, 128), BF16),
            vmem((T, 3 * HW), BF16),
            vmem((T // 2, D), F32),
            vmem((T // 2, D), F32),
            vmem((16, 16, D), BF16),
            vmem((16, 16, D), BF16),
            vmem((2, 3, 4, 96, D), BF16),
            vmem((2, 3, 3, 96, D), BF16),
            vmem((2, 3, 4, 32, D), BF16),
            vmem((2, 3, 3, 32, D), BF16),
            vmem((2, 3, 4, 16, D), BF16),
            vmem((2, 3, 3, 16, D), BF16),
            vmem((2, 2, 16, D), F32),
            vmem((2, 16, D), F32),
            dma((2, 16)),
            dma((2, 32)),
            dma((2, 16)),
            dma((2,)),
            dma((4,)),
            dma((2,)),
            dma((2,)),
            dma((2, 16)),
            dma((2, 16)),
            dma((2, 3, 3)),
            dma((2, 3, 3)),
            dma((2, 3, 3)),
            dma((2, 3, 3)),
            dma((2, 3, 3)),
            dma((2, 3, 3)),
            dma((2,)),
            dma((2,)),
        ],
        compiler_params=pltpu.CompilerParams(
            collective_id=0, has_side_effects=True, vmem_limit_bytes=VMEM_LIMIT
        ),
    )(*operands)


def on_device(latents, shift_mod, scale_mod, gate_mod, qkv_weight, out_weight, cotangent):
    bo, lg, qkvg, outg = run_block(
        latents[0], cotangent[0], shift_mod, scale_mod, gate_mod, qkv_weight, out_weight
    )
    return bo[None], lg[None], qkvg, outg


def solution(mesh):
    in_specs = (
        P("dp", None, "seq", None),
        P("dp", None),
        P("dp", None),
        P("dp", None),
        P(),
        P(),
        P("dp", None, "seq", None),
    )
    out_specs = (
        P("dp", None, "seq", None),
        P("dp", None, "seq", None),
        P(("dp", "seq"), None),
        P(("dp", "seq"), None),
    )
    return jax.shard_map(
        on_device, mesh=mesh, in_specs=in_specs, out_specs=out_specs, check_vma=False
    )
```
